32 devices in a mesh: row: 8 (over z, x), col: 4 (over y, core).
Axes of the slice: x: 2, y: 2, z: 4, core: 2. Of those that a mesh axis runs over, the one named last changes fastest.
Arguments:
- front_base: float32 [16, 8, 128, 32, 4, 128], P(None, 'row', None, None, 'col')
- traces: bfloat16 [16, 8, 4, 3, 128, 128], P(None, 'row'), may hold values from -0.75 to 0.75
- adjacency: int32 [128, 4], replicated, may hold values from 0 to 127, as said below
- pivot_order: int32 [2, 512], replicated, may hold values from 0 to 511, each once within a row
- pivot_kind: int32 [2, 512], replicated, may hold values from 0 to 2, as said below
- inverse_diagonal: float32 [2, 512], replicated, may hold values from -0.3 to 0.3
- inverse_coupling: float32 [2, 512], replicated, may hold values from -0.3 to 0.3
- readers: int32 [2, 128], replicated, may hold values 0 or 1
Outputs:
- trailing: float32 [16, 8, 128, 32, 4, 128], P(None, 'row', None, None, 'col')
The draws below stay inside these ranges and needn't reach their ends.
Inputs may be any that keep to these rules, and one draw needn't show every extreme that they name: The elements form a 16 x 8 grid that closes on itself in both dimensions, numbered in a drawn order; faces 0 and 1 lead to the next and previous element along the first dimension, 2 and 3 along the second, so adjacency[adjacency[e, f], f with its lowest bit flipped] = e. `pivot_kind`: 0 marks a 1 x 1 pivot; 1 marks the first position of a 2 x 2 pivot, whose second position follows and is marked 2; 2 x 2 pivots start at even positions.
All inputs are finite; a program needn't handle non-finite values.
Results may differ from the reference program's by a relative error of at most 0.008.
Values may be sent and summed in bfloat16 or wider, within the bound.
A program may use at most 256 MiB of HBM per device.

```python
import jax
import jax.numpy as jnp

NB = 128
Q = 128
E = 128
EGY = 8
PW = 512
PANELS = 2
RB = 16
N_ROW = 8
N_COL = 4


def draw_front_base(key, part):
    front_order = E * NB
    entries = jax.random.normal(key, (front_order, front_order), jnp.float32)
    symmetric = (entries + entries.T) * 0.7071
    return symmetric.reshape(E // N_ROW, N_ROW, NB, E // N_COL, N_COL, NB)


def draw_adjacency(key, part):
    element_ids = jax.random.permutation(key, E).astype(jnp.int32)
    element_grid = element_ids.reshape(E // EGY, EGY)
    neighbours = jnp.stack([jnp.roll(element_grid, -1, 0), jnp.roll(element_grid, 1, 0), jnp.roll(element_grid, -1, 1), jnp.roll(element_grid, 1, 1)], axis=-1).reshape(E, 4)
    return jnp.zeros((E, 4), jnp.int32).at[element_grid.reshape(E)].set(neighbours)


def draw_pivot_kind(key, part):
    pair_flags = jax.random.randint(key, (PANELS, PW // 2), 0, 2).astype(jnp.int32)
    return jnp.stack([pair_flags, 2 * pair_flags], axis=-1).reshape(PANELS, PW)


def plant(values, rng, low, high):
    extent = values.shape
    index_at = [jax.random.randint(jax.random.fold_in(rng, axis), (), 0, extent[axis]) for axis in range(len(extent))]
    values = values.at[tuple(index_at)].set(low)
    longest = extent.index(max(extent))
    index_at[longest] = (index_at[longest] + 1) % extent[longest]
    return values.at[tuple(index_at)].set(high)


def steps_of(rng, extent, split, low, high):
    loudness, own = 1.0, jax.random.fold_in(rng, 6)
    for dim, blocks in split:
        heights = jnp.exp(jax.random.uniform(jax.random.fold_in(own, dim), (blocks,), jnp.float32, low / len(split), high / len(split)))
        loudness = loudness * jnp.repeat(heights, extent[dim] // blocks).reshape([-1 if axis == dim else 1 for axis in range(len(extent))])
    return loudness


def centred(rng, shape, deviation, limit, pieces=(), kind=jnp.bfloat16):
    drawn = deviation * jax.random.normal(rng, shape, jnp.float32)
    if pieces:
        drawn = drawn * steps_of(rng, shape, pieces, -0.22, 0.18)
    return jnp.clip(drawn, -limit, limit).astype(kind)


def setup_inputs(seed: int = 0) -> dict:
    seeds = jax.random.split(jax.random.key(seed), 9)
    front_base = draw_front_base(jax.random.fold_in(seeds[8], 71), 0)
    traces = centred(seeds[1], (RB, N_ROW, 4, 3, Q, NB), 0.125, 0.75, ((1, 8),))
    adjacency = draw_adjacency(jax.random.fold_in(seeds[8], 71), 0)
    pivot_order = jax.vmap(lambda own: jax.random.permutation(own, PW))(jax.random.split(seeds[3], PANELS)).reshape((PANELS, PW)).astype(jnp.int32)
    pivot_kind = draw_pivot_kind(jax.random.fold_in(seeds[8], 71), 0)
    inverse_diagonal = centred(seeds[5], (PANELS, PW), 0.05, 0.3, (), jnp.float32)
    inverse_coupling = centred(seeds[6], (PANELS, PW), 0.05, 0.3, (), jnp.float32)
    readers = plant((jax.random.randint(seeds[7], (PANELS, E), 0, 4) < 3).astype(jnp.int32), jax.random.fold_in(seeds[7], 1), 0, 1)
    return {"front_base": front_base, "traces": traces, "adjacency": adjacency, "pivot_order": pivot_order, "pivot_kind": pivot_kind, "inverse_diagonal": inverse_diagonal, "inverse_coupling": inverse_coupling, "readers": readers}


def face_left(values):
    return jnp.concatenate([values[:, :, 0], values[:, :, 0], values[:, :, 1], values[:, :, 2]], axis=2)


def face_right(values):
    return jnp.concatenate([4.0 * values[:, :, 0], -0.5 * values[:, :, 1], -0.5 * values[:, :, 0], 2.0 * values[:, :, 2]], axis=2)


def apply_inverse(values, pivot_kinds, diagonal, pair_terms):
    starts = (pivot_kinds == 1).astype(values.dtype)
    upward = pair_terms * starts
    upward_prev = jnp.concatenate([jnp.zeros_like(upward[:1]), upward[:-1]])
    following = jnp.concatenate([values[:, 1:], jnp.zeros_like(values[:, :1])], axis=1)
    preceding = jnp.concatenate([jnp.zeros_like(values[:, :1]), values[:, :-1]], axis=1)
    return values * diagonal + following * upward + preceding * upward_prev


def reference(front_base, traces, adjacency, pivot_order, pivot_kind, inverse_diagonal, inverse_coupling, readers):
    front_order = E * NB
    element_traces = traces.reshape(E, 4, 3, Q, NB)
    left_parts = face_left(element_traces).astype(jnp.float32)
    right_parts = face_right(element_traces).astype(jnp.float32)
    opposite = jnp.array([1, 0, 3, 2], dtype=jnp.int32)
    partner = right_parts[adjacency, opposite[None, :]]
    coupling = jnp.einsum("efqi,efqj->efij", left_parts, partner)
    self_terms = jnp.einsum("efqi,efqj->eij", left_parts, right_parts)
    blocks = front_base.reshape(E, NB, E, NB)
    rows_index = jnp.broadcast_to(jnp.arange(E, dtype=jnp.int32)[:, None], (E, 4))
    blocks = blocks.at[rows_index, :, adjacency, :].add(-coupling)
    diag_index = jnp.arange(E, dtype=jnp.int32)
    blocks = blocks.at[diag_index, :, diag_index, :].add(self_terms)
    front_mat = blocks.reshape(front_order, front_order)
    block_id = jnp.arange(E, dtype=jnp.int32)
    for which_panel in range(PANELS):
        first_col = which_panel * PW
        columns = front_mat[:, first_col:first_col + PW].astype(jnp.bfloat16)
        columns = jnp.take(columns, pivot_order[which_panel], axis=1)
        kept_blocks = readers[which_panel] * (block_id >= (first_col + PW) // NB).astype(jnp.int32)
        kept_rows = jnp.repeat(kept_blocks, NB).astype(jnp.bfloat16)
        panel_vals = columns * kept_rows[:, None]
        scaled = apply_inverse(panel_vals.astype(jnp.float32), pivot_kind[which_panel], inverse_diagonal[which_panel], inverse_coupling[which_panel]).astype(jnp.bfloat16)
        front_mat = front_mat - jnp.dot(scaled, panel_vals.T, preferred_element_type=jnp.float32)
    return front_mat.reshape(E // N_ROW, N_ROW, NB, E // N_COL, N_COL, NB)
```

```python
import functools

import jax
import jax.numpy as jnp
from jax import lax
from jax.experimental import pallas as pl
from jax.experimental.pallas import tpu as pltpu
from jax.sharding import PartitionSpec as P

NB = 128
PW = 512
PANELS = 2
PB = PW // NB
MESH = pl.DeviceIdType.MESH
VMEM_LIMIT = 56 * 1024 * 1024
F32, BF16 = jnp.float32, jnp.bfloat16


def gather_kernel(rows, cols, split, keep_row, *refs):
    if keep_row:
        x_ref, g_ref, l_ref, swap_send, swap_recv, ring_send, ring_recv, row_send, row_recv = refs
    else:
        x_ref, g_ref, swap_send, swap_recv, ring_send, ring_recv = refs
    r, c = lax.axis_index("row"), lax.axis_index("col")
    s = lax.rem(r, cols)
    peer_row = r - s + c
    peer = (peer_row, s)
    stays = s == c

    def row_at(p):
        p = lax.rem(p + 2 * rows, rows)
        up = lax.div(p, rows // 2)
        return (1 - up) * (2 * p) + up * (2 * (rows - 1 - p) + 1)

    odd = lax.rem(r, 2)
    pos = (1 - odd) * lax.div(r, 2) + odd * (rows - 1 - lax.div(r, 2))
    beside = ((row_at(pos + 1), c), (row_at(pos - 1), c))

    barrier = pltpu.get_barrier_semaphore()
    for device in beside:
        pl.semaphore_signal(barrier, inc=1, device_id=device, device_id_type=MESH)
    greeted = 2
    if keep_row:
        for j in range(1, cols):
            pl.semaphore_signal(
                barrier, inc=1, device_id=(r, lax.rem(c + j, cols)), device_id_type=MESH
            )
        greeted += cols - 1

    @pl.when(jnp.logical_not(stays))
    def _():
        pl.semaphore_signal(barrier, inc=1, device_id=peer, device_id_type=MESH)
        pl.semaphore_wait(barrier, greeted + 1)

    @pl.when(stays)
    def _():
        pl.semaphore_wait(barrier, greeted)

    def source(half):
        return x_ref.at[c, half] if split else x_ref.at[half]

    def swap(half, slot):
        return pltpu.make_async_remote_copy(
            src_ref=source(half), dst_ref=g_ref.at[slot, half], send_sem=swap_send.at[half],
            recv_sem=swap_recv.at[half], device_id=peer, device_id_type=MESH,
        )

    def keep(half):
        return pltpu.make_async_copy(source(half), g_ref.at[r, half], swap_recv.at[half])

    @pl.when(stays)
    def _():
        for half in range(2):
            keep(half).start()

    @pl.when(jnp.logical_not(stays))
    def _():
        for half in range(2):
            swap(half, peer_row).start()

    def along_row(j, slot):
        return pltpu.make_async_remote_copy(
            src_ref=x_ref, dst_ref=l_ref.at[slot], send_sem=row_send.at[j], recv_sem=row_recv.at[j],
            device_id=(r, lax.rem(c + j, cols)), device_id_type=MESH,
        )

    if keep_row:
        own = pltpu.make_async_copy(x_ref, l_ref.at[c], row_recv.at[0])
        own.start()
        for j in range(1, cols):
            along_row(j, c).start()

    def ring(way, step):
        origin = row_at(pos - step) if way == 0 else row_at(pos + step)
        return pltpu.make_async_remote_copy(
            src_ref=g_ref.at[origin, way], dst_ref=g_ref.at[origin, way],
            send_sem=ring_send.at[way, step], recv_sem=ring_recv.at[way, step],
            device_id=beside[way], device_id_type=MESH,
        )

    def arrived(way, step):
        origin = row_at(pos - step - 1) if way == 0 else row_at(pos + step + 1)
        return pltpu.make_async_remote_copy(
            src_ref=g_ref.at[origin, way], dst_ref=g_ref.at[origin, way],
            send_sem=ring_send.at[way, step], recv_sem=ring_recv.at[way, step],
            device_id=beside[way], device_id_type=MESH,
        )

    for way in range(2):

        @pl.when(stays)
        def _():
            keep(way).wait()

        @pl.when(jnp.logical_not(stays))
        def _():
            swap(way, r).wait_recv()

        ring(way, 0).start()
    for step in range(1, rows - 1):
        for way in range(2):
            arrived(way, step - 1).wait_recv()
            ring(way, step).start()
    for way in range(2):
        arrived(way, rows - 2).wait_recv()
    for step in range(rows - 1):
        for way in range(2):
            ring(way, step).wait_send()

    @pl.when(jnp.logical_not(stays))
    def _():
        for half in range(2):
            swap(half, peer_row).wait_send()

    if keep_row:
        own.wait()
        for j in range(1, cols):
            along_row(j, lax.rem(c + cols - j, cols)).wait_recv()
            along_row(j, c).wait_send()


def gather(x, rows, cols, split, keep_row, identity):
    piece = x.shape[1:] if split else x.shape
    out_shape = [jax.ShapeDtypeStruct((rows,) + piece, x.dtype)]
    dma = pltpu.SemaphoreType.DMA
    scratch = [dma((2,)), dma((2,)), dma((2, rows - 1)), dma((2, rows - 1))]
    if keep_row:
        out_shape.append(jax.ShapeDtypeStruct((cols,) + piece, x.dtype))
        scratch += [dma((cols,)), dma((cols,))]
    moved = 2 * sum(o.size for o in out_shape)
    return pl.pallas_call(
        functools.partial(gather_kernel, rows, cols, split, keep_row),
        out_shape=out_shape,
        in_specs=[pl.BlockSpec(memory_space=pl.ANY)],
        out_specs=[pl.BlockSpec(memory_space=pl.ANY)] * len(out_shape),
        scratch_shapes=scratch,
        compiler_params=pltpu.CompilerParams(collective_id=identity, has_side_effects=True),
        cost_estimate=pl.CostEstimate(flops=0, bytes_accessed=20 * moved, transcendentals=0),
    )(x)


def face_kernel(slots, held, partner, self_info, own_ref, p0, p1, p2, p3, a_ref, c_ref, s_ref, v_ref, acc):
    e = pl.program_id(0)
    panel_slots = acc.shape[1] // NB
    acc[...] = a_ref[0]
    contract = (((0,), (0,)), ((), ()))

    def left(f):
        v, s, l = own_ref[0, f, 0], own_ref[0, f, 1], own_ref[0, f, 2]
        return jnp.concatenate([v, v, s, l], axis=0)

    def right(v, s, l):
        return jnp.concatenate([4.0 * v, -0.5 * s, -0.5 * v, 2.0 * l], axis=0)

    for f, p_ref in enumerate((p0, p1, p2, p3)):

        @pl.when(held[e * 4 + f] == 1)
        def _():
            z = right(p_ref[0, 0], p_ref[0, 1], p_ref[0, 2])
            c_ref[0, f] = lax.dot_general(left(f), z, contract, preferred_element_type=F32)
            for j in range(panel_slots):

                @pl.when(slots[e * 4 + f] == j)
                def _():
                    acc[:, j * NB : (j + 1) * NB] -= c_ref[0, f]

    @pl.when(self_info[0] == 1)
    def _():
        total = jnp.zeros((NB, NB), F32)
        for f in range(4):
            z = right(own_ref[0, f, 0], own_ref[0, f, 1], own_ref[0, f, 2])
            total += lax.dot_general(left(f), z, contract, preferred_element_type=F32)
        s_ref[0] = total
        for j in range(panel_slots):

            @pl.when(self_info[1 + e] == j)
            def _():
                acc[:, j * NB : (j + 1) * NB] += total

    v_ref[0] = acc[...].astype(BF16)


def faces(traces, partners, base, slots, held, partner, self_info):
    row_blocks, width = base.shape[0], base.shape[2]
    in_specs = [pl.BlockSpec((1, 4, 3, NB, NB), lambda e, *_: (e, 0, 0, 0, 0))]
    for f in range(4):
        in_specs.append(
            pl.BlockSpec((1, 3, NB, NB), lambda e, s, h, p, i, f=f: (p[e * 4 + f], 0, 0, 0))
        )
    in_specs.append(pl.BlockSpec((1, NB, width), lambda e, *_: (e, 0, 0)))
    return pl.pallas_call(
        face_kernel,
        grid_spec=pltpu.PrefetchScalarGridSpec(
            num_scalar_prefetch=4,
            grid=(row_blocks,),
            in_specs=in_specs,
            out_specs=[
                pl.BlockSpec((1, 4, NB, NB), lambda e, *_: (e, 0, 0, 0)),
                pl.BlockSpec((1, NB, NB), lambda e, *_: (e, 0, 0)),
                pl.BlockSpec((1, NB, width), lambda e, *_: (e, 0, 0)),
            ],
            scratch_shapes=[pltpu.VMEM((NB, width), F32)],
        ),
        out_shape=[
            jax.ShapeDtypeStruct((row_blocks, 4, NB, NB), F32),
            jax.ShapeDtypeStruct((row_blocks, NB, NB), F32),
            jax.ShapeDtypeStruct((row_blocks, NB, width), BF16),
        ],
        compiler_params=pltpu.CompilerParams(vmem_limit_bytes=VMEM_LIMIT),
    )(slots, held, partner, self_info, traces, partners, partners, partners, partners, base)


def panel_kernel(cols, transposed, kept, raw_ref, hi_ref, lo_ref, pivot_ref, out_ref):
    q, t = pl.program_id(0), pl.program_id(1)
    per = raw_ref.shape[2]
    blocks = pl.num_programs(1) * per
    first = q * blocks + t * per
    count = pl.num_programs(0) * blocks

    def masked(k, parts):
        return jnp.concatenate(
            [
                jnp.where(kept[k * count + first + i] == 1, parts[i], jnp.zeros_like(parts[i]))
                for i in range(per)
            ],
            axis=0,
        )

    def raw(k, i):
        pieces = []
        for b in range(k * PB, (k + 1) * PB):
            at = (b // cols) * NB
            pieces.append(raw_ref[0, b % cols, i, :, at : at + NB])
        return jnp.concatenate(pieces, axis=1)

    def scaled(k, v):
        w = jnp.dot(v, hi_ref[k], preferred_element_type=F32)
        return (w + jnp.dot(v, lo_ref[k], preferred_element_type=F32)).astype(BF16)

    v0 = masked(0, [raw(0, i) for i in range(per)])
    w0 = scaled(0, v0)
    taken = jnp.dot(w0, pivot_ref[...], preferred_element_type=F32)
    v1 = masked(
        1,
        [
            (raw(1, i).astype(F32) - taken[i * NB : (i + 1) * NB]).astype(BF16)
            for i in range(per)
        ],
    )
    if transposed:
        out_ref[:PW, :] = v0.T
        out_ref[PW:, :] = v1.T
    else:
        out_ref[:, :PW] = w0
        out_ref[:, PW:] = scaled(1, v1)


def panels(raw, kept, hi, lo, pivot_rows, transposed):
    groups, cols, row_blocks, _, width = raw.shape
    per = 4
    steps = row_blocks // per
    total = groups * row_blocks * NB
    whole = lambda shape: pl.BlockSpec(shape, lambda q, t, *_: (0,) * len(shape))
    if transposed:
        shape = (PANELS * PW, total)
        out_spec = pl.BlockSpec((PANELS * PW, per * NB), lambda q, t, *_: (0, q * steps + t))
    else:
        shape = (total, PANELS * PW)
        out_spec = pl.BlockSpec((per * NB, PANELS * PW), lambda q, t, *_: (q * steps + t, 0))
    return pl.pallas_call(
        functools.partial(panel_kernel, cols, transposed),
        grid_spec=pltpu.PrefetchScalarGridSpec(
            num_scalar_prefetch=1,
            grid=(groups, steps),
            in_specs=[
                pl.BlockSpec((1, cols, per, NB, width), lambda q, t, *_: (q, 0, t, 0, 0)),
                whole(hi.shape),
                whole(lo.shape),
                whole(pivot_rows.shape),
            ],
            out_specs=out_spec,
        ),
        out_shape=jax.ShapeDtypeStruct(shape, BF16),
        compiler_params=pltpu.CompilerParams(vmem_limit_bytes=VMEM_LIMIT),
    )(kept, raw, hi, lo, pivot_rows)


def update_kernel(groups, col_blocks, per, slots, held, self_info, a_ref, w_ref, v_ref, c_ref, s_ref, o_ref):
    t = pl.program_id(0)
    rows = per * NB
    per_group = col_blocks // groups
    w = w_ref[...]
    for h in range(groups):
        for a in range(0, per_group, 2):
            at = (h * per_group + a) * NB
            acc = jnp.dot(w, v_ref[:, at : at + 2 * NB], preferred_element_type=F32)
            for k in range(2):
                here = pl.ds((a + k) * groups + h, rows, stride=col_blocks)
                o_ref[here, :] = a_ref[here, :] - acc[:, k * NB : (k + 1) * NB]
    for i in range(per):
        e = t * per + i
        for f in range(4):

            @pl.when(held[e * 4 + f] == 1)
            def _():
                here = pl.ds(i * NB * col_blocks + slots[e * 4 + f], NB, stride=col_blocks)
                o_ref[here, :] = o_ref[here, :] - c_ref[i, f]

        @pl.when(self_info[0] == 1)
        def _():
            here = pl.ds(i * NB * col_blocks + self_info[1 + e], NB, stride=col_blocks)
            o_ref[here, :] = o_ref[here, :] + s_ref[i]


def update(front, w, v, coupling, self_terms, slots, held, self_info, groups, col_blocks):
    per = 2
    row_blocks = coupling.shape[0]
    wide = per * NB * col_blocks
    return pl.pallas_call(
        functools.partial(update_kernel, groups, col_blocks, per),
        grid_spec=pltpu.PrefetchScalarGridSpec(
            num_scalar_prefetch=3,
            grid=(row_blocks // per,),
            in_specs=[
                pl.BlockSpec((wide, NB), lambda t, *_: (t, 0)),
                pl.BlockSpec((per * NB, PANELS * PW), lambda t, *_: (t, 0)),
                pl.BlockSpec(v.shape, lambda t, *_: (0, 0)),
                pl.BlockSpec((per, 4, NB, NB), lambda t, *_: (t, 0, 0, 0)),
                pl.BlockSpec((per, NB, NB), lambda t, *_: (t, 0, 0)),
            ],
            out_specs=pl.BlockSpec((wide, NB), lambda t, *_: (t, 0)),
        ),
        out_shape=jax.ShapeDtypeStruct(front.shape, F32),
        compiler_params=pltpu.CompilerParams(vmem_limit_bytes=VMEM_LIMIT),
    )(slots, held, self_info, front, w, v, coupling, self_terms)


def inverse_matrix(order, kinds, diagonal, pair_terms):
    ids = jnp.arange(PW, dtype=jnp.int32)
    hot = order[:, :, None] == ids
    place = jnp.sum(jnp.where(hot, ids[None, :, None], 0), axis=1)
    diag = jnp.sum(jnp.where(hot, diagonal[:, :, None], 0.0), axis=1)
    starts = jnp.where(kinds == 1, pair_terms, 0.0)
    pair = jnp.sum(jnp.where(hot, starts[:, :, None], 0.0), axis=1)
    row, col = place[:, :, None], place[:, None, :]
    full = jnp.where(row == col, diag[:, :, None], 0.0)
    full = full + jnp.where(col == row + 1, pair[:, :, None], 0.0)
    full = full + jnp.where(row == col + 1, pair[:, None, :], 0.0)
    hi = full.astype(BF16)
    return hi, (full - hi.astype(F32)).astype(BF16)


def local(
    front_base,
    traces,
    adjacency,
    pivot_order,
    pivot_kind,
    inverse_diagonal,
    inverse_coupling,
    readers,
):
    rows, cols = lax.axis_size("row"), lax.axis_size("col")
    r, c = lax.axis_index("row"), lax.axis_index("col")
    row_blocks, col_blocks = front_base.shape[0], front_base.shape[3]
    groups = rows // cols
    panel_slots = -(-PANELS * PB // cols)
    width = panel_slots * NB

    own = traces.reshape(row_blocks, 4, 3, NB, NB)
    share = row_blocks * 4 // cols
    sent = traces.reshape(cols, 2, share // 2, 3 * NB, NB)
    (column_traces,) = gather(sent, rows, cols, True, False, 0)
    partners = column_traces.reshape(groups * row_blocks * 4, 3, NB, NB)

    elements = jnp.arange(row_blocks, dtype=jnp.int32) * rows + r
    neighbour = jnp.take(adjacency, elements, axis=0)
    opposite = jnp.array([1, 0, 3, 2], dtype=jnp.int32)
    here = neighbour % cols == c
    slots = (neighbour // cols).reshape(-1)
    partner = ((neighbour % rows // cols) * row_blocks + neighbour // rows) * 4 + opposite
    partner = jnp.where(here, partner, 0).reshape(-1)
    held = here.astype(jnp.int32).reshape(-1)
    self_here = (r % cols == c).astype(jnp.int32)
    self_info = jnp.concatenate([self_here[None], elements // cols])

    base = front_base[:, 0, :, :panel_slots, 0, :].reshape(row_blocks, NB, width)
    coupling, self_terms, raw = faces(own, partners, base, slots, held, partner, self_info)

    every = lax.all_gather(raw[0, :, :NB], ("row", "col"), axis=0, tiled=False)
    column_raw, row_raw = gather(
        raw.reshape(2, row_blocks * NB // 2, width), rows, cols, False, True, 1
    )
    ids = jnp.arange(rows * row_blocks, dtype=jnp.int32)
    kept = jnp.stack(
        [readers[k] * (ids >= (k + 1) * PB).astype(jnp.int32) for k in range(PANELS)]
    )
    by_row = kept.reshape(PANELS, row_blocks, rows)
    row_kept = lax.dynamic_index_in_dim(by_row, r, 2, keepdims=False)
    by_col = kept.reshape(PANELS, row_blocks, groups, cols)
    col_kept = lax.dynamic_index_in_dim(by_col, c, 3, keepdims=False).transpose(0, 2, 1)

    pivot = every.reshape(rows, cols, NB, NB)[PB : 2 * PB, :PB]
    pivot = pivot * kept[0, PB : 2 * PB].astype(BF16)[:, None, None, None]
    pivot_rows = pivot.transpose(1, 3, 0, 2).reshape(PW, PW)
    hi, lo = inverse_matrix(pivot_order, pivot_kind, inverse_diagonal, inverse_coupling)
    shape = (cols, row_blocks, NB, width)
    w = panels(row_raw.reshape((1,) + shape), row_kept.reshape(-1), hi, lo, pivot_rows, False)
    v = panels(column_raw.reshape((groups,) + shape), col_kept.reshape(-1), hi, lo, pivot_rows, True)

    front = front_base.reshape(row_blocks * NB * col_blocks, NB)
    out = update(front, w, v, coupling, self_terms, slots, held, self_info, groups, col_blocks)
    return out.reshape(front_base.shape)


def solution(mesh):
    in_specs = (
        P(None, "row", None, None, "col", None),
        P(None, "row", None, None, None, None),
        P(),
        P(),
        P(),
        P(),
        P(),
        P(),
    )
    out_specs = P(None, "row", None, None, "col", None)
    return jax.shard_map(local, mesh=mesh, in_specs=in_specs, out_specs=out_specs, check_vma=False)
```

```python
import functools

import jax
import jax.numpy as jnp
from jax import lax
from jax.experimental import pallas as pl
from jax.experimental.pallas import tpu as pltpu
from jax.sharding import PartitionSpec as P

NB = 128
PW = 512
PANELS = 2
PB = PW // NB
MESH = pl.DeviceIdType.MESH
VMEM_LIMIT = 56 * 1024 * 1024
F32, BF16 = jnp.float32, jnp.bfloat16


def gather_kernel(rows, cols, parts, split, keep_row, *refs):
    if keep_row:
        (x_ref, y_ref, g_ref, l_ref, t_ref, swap_send, swap_recv, ring_send, ring_recv,
         row_send, row_recv, turn_send, turn_recv) = refs
    else:
        x_ref, g_ref, swap_send, swap_recv, ring_send, ring_recv = refs
    groups = rows // cols
    r, c = lax.axis_index("row"), lax.axis_index("col")
    s = lax.rem(r, cols)
    h = lax.div(r, cols)
    peer_row = r - s + c
    peer = (peer_row, s)
    stays = s == c

    def row_at(p):
        p = lax.rem(p + 2 * rows, rows)
        up = lax.div(p, rows // 2)
        return (1 - up) * (2 * p) + up * (2 * (rows - 1 - p) + 1)

    odd = lax.rem(r, 2)
    pos = (1 - odd) * lax.div(r, 2) + odd * (rows - 1 - lax.div(r, 2))
    beside = ((row_at(pos + 1), c), (row_at(pos - 1), c))
    pieces = [(way, part) for part in range(parts) for way in range(2)]

    barrier = pltpu.get_barrier_semaphore()
    for device in beside:
        pl.semaphore_signal(barrier, inc=1, device_id=device, device_id_type=MESH)
    greeted = 2
    if keep_row:
        for j in range(1, cols):
            pl.semaphore_signal(
                barrier, inc=1, device_id=(r, lax.rem(c + j, cols)), device_id_type=MESH
            )
        for j in range(1, groups):
            turned = lax.rem(h + j, groups) * cols + c
            pl.semaphore_signal(barrier, inc=1, device_id=(turned, s), device_id_type=MESH)
        greeted += cols - 1 + groups - 1

    @pl.when(jnp.logical_not(stays))
    def _():
        pl.semaphore_signal(barrier, inc=1, device_id=peer, device_id_type=MESH)
        pl.semaphore_wait(barrier, greeted + 1)

    @pl.when(stays)
    def _():
        pl.semaphore_wait(barrier, greeted)

    def source(way, part):
        return x_ref.at[c, way, part] if split else x_ref.at[way, part]

    def swap(way, part, slot):
        return pltpu.make_async_remote_copy(
            src_ref=source(way, part), dst_ref=g_ref.at[slot, way, part],
            send_sem=swap_send.at[way, part], recv_sem=swap_recv.at[way, part],
            device_id=peer, device_id_type=MESH,
        )

    def keep(way, part):
        return pltpu.make_async_copy(
            source(way, part), g_ref.at[r, way, part], swap_recv.at[way, part]
        )

    @pl.when(stays)
    def _():
        for piece in pieces:
            keep(*piece).start()

    @pl.when(jnp.logical_not(stays))
    def _():
        for piece in pieces:
            swap(*piece, peer_row).start()

    def along_row(j, slot):
        return pltpu.make_async_remote_copy(
            src_ref=x_ref, dst_ref=l_ref.at[slot], send_sem=row_send.at[j], recv_sem=row_recv.at[j],
            device_id=(r, lax.rem(c + j, cols)), device_id_type=MESH,
        )

    def turn(j, slot):
        k = lax.rem(h + j, groups)
        return pltpu.make_async_remote_copy(
            src_ref=y_ref.at[k], dst_ref=t_ref.at[slot], send_sem=turn_send.at[j],
            recv_sem=turn_recv.at[j], device_id=(k * cols + c, s), device_id_type=MESH,
        )

    def turn_kept():
        return pltpu.make_async_copy(y_ref.at[h], t_ref.at[h], turn_recv.at[0])

    if keep_row:
        own = pltpu.make_async_copy(x_ref, l_ref.at[c], row_recv.at[0])
        own.start()
        for j in range(1, cols):
            along_row(j, c).start()
        for j in range(1, groups):
            turn(j, h).start()

        @pl.when(stays)
        def _():
            turn_kept().start()

        @pl.when(jnp.logical_not(stays))
        def _():
            turn(0, h).start()

    def ring(way, part, step, behind):
        origin = row_at(pos - step - behind) if way == 0 else row_at(pos + step + behind)
        return pltpu.make_async_remote_copy(
            src_ref=g_ref.at[origin, way, part], dst_ref=g_ref.at[origin, way, part],
            send_sem=ring_send.at[way, part, step], recv_sem=ring_recv.at[way, part, step],
            device_id=beside[way], device_id_type=MESH,
        )

    for way, part in pieces:

        @pl.when(stays)
        def _():
            keep(way, part).wait()

        @pl.when(jnp.logical_not(stays))
        def _():
            swap(way, part, r).wait_recv()

        ring(way, part, 0, 0).start()
    for step in range(1, rows - 1):
        for way, part in pieces:
            ring(way, part, step - 1, 1).wait_recv()
            ring(way, part, step, 0).start()
    for way, part in pieces:
        ring(way, part, rows - 2, 1).wait_recv()
    for step in range(rows - 1):
        for way, part in pieces:
            ring(way, part, step, 0).wait_send()

    @pl.when(jnp.logical_not(stays))
    def _():
        for piece in pieces:
            swap(*piece, peer_row).wait_send()

    if keep_row:
        own.wait()
        for j in range(1, cols):
            along_row(j, lax.rem(c + cols - j, cols)).wait_recv()
            along_row(j, c).wait_send()
        for j in range(1, groups):
            turn(j, lax.rem(h + groups - j, groups)).wait_recv()
            turn(j, h).wait_send()

        @pl.when(stays)
        def _():
            turn_kept().wait()

        @pl.when(jnp.logical_not(stays))
        def _():
            turn(0, h).wait_recv()
            turn(0, h).wait_send()


def gather(x, rows, cols, split, identity, turned=None):
    piece = x.shape[1:] if split else x.shape
    parts = piece[1]
    out_shape = [jax.ShapeDtypeStruct((rows,) + piece, x.dtype)]
    dma = pltpu.SemaphoreType.DMA
    scratch = [dma((2, parts)), dma((2, parts)), dma((2, parts, rows - 1)), dma((2, parts, rows - 1))]
    operands = [x]
    keep_row = turned is not None
    if keep_row:
        out_shape.append(jax.ShapeDtypeStruct((cols,) + piece, x.dtype))
        out_shape.append(jax.ShapeDtypeStruct(turned.shape, turned.dtype))
        scratch += [dma((cols,)), dma((cols,)), dma((rows // cols,)), dma((rows // cols,))]
        operands.append(turned)
    moved = 2 * sum(o.size for o in out_shape)
    return pl.pallas_call(
        functools.partial(gather_kernel, rows, cols, parts, split, keep_row),
        out_shape=out_shape,
        in_specs=[pl.BlockSpec(memory_space=pl.ANY)] * len(operands),
        out_specs=[pl.BlockSpec(memory_space=pl.ANY)] * len(out_shape),
        scratch_shapes=scratch,
        compiler_params=pltpu.CompilerParams(collective_id=identity, has_side_effects=True),
        cost_estimate=pl.CostEstimate(flops=0, bytes_accessed=20 * moved, transcendentals=0),
    )(*operands)


def face_kernel(slots, held, partner, self_info, place, own_ref, p0, p1, p2, p3, a_ref, c_ref, s_ref, v_ref, t_ref, acc):
    e = pl.program_id(0)
    panel_slots = acc.shape[1] // NB
    acc[...] = a_ref[0]
    contract = (((0,), (0,)), ((), ()))

    def left(f):
        v, s, l = own_ref[0, f, 0], own_ref[0, f, 1], own_ref[0, f, 2]
        return jnp.concatenate([v, v, s, l], axis=0)

    def right(v, s, l):
        return jnp.concatenate([4.0 * v, -0.5 * s, -0.5 * v, 2.0 * l], axis=0)

    @pl.when(e == 0)
    def _():
        t_ref[...] = jnp.zeros_like(t_ref)

    for f, p_ref in enumerate((p0, p1, p2, p3)):
        wanted = held[e * 4 + f] == 1
        if f % 2:
            wanted = jnp.logical_and(wanted, slots[e * 4 + f] < panel_slots)

        @pl.when(wanted)
        def _():
            z = right(p_ref[0, 0], p_ref[0, 1], p_ref[0, 2])
            block = lax.dot_general(left(f), z, contract, preferred_element_type=F32)
            if f % 2 == 0:
                c_ref[0, f // 2] = block

                @pl.when(place[e * 2 + f // 2] >= 0)
                def _():
                    t_ref[place[e * 2 + f // 2]] = block.T.astype(BF16)

            for j in range(panel_slots):

                @pl.when(slots[e * 4 + f] == j)
                def _():
                    acc[:, j * NB : (j + 1) * NB] -= block

    @pl.when(self_info[0] == 1)
    def _():
        total = jnp.zeros((NB, NB), F32)
        for f in range(4):
            z = right(own_ref[0, f, 0], own_ref[0, f, 1], own_ref[0, f, 2])
            total += lax.dot_general(left(f), z, contract, preferred_element_type=F32)
        s_ref[0] = total
        for j in range(panel_slots):

            @pl.when(self_info[1 + e] == j)
            def _():
                acc[:, j * NB : (j + 1) * NB] += total

    v_ref[0] = acc[...].astype(BF16)


def faces(traces, partners, base, slots, held, partner, self_info, place, room):
    row_blocks, width = base.shape[0], base.shape[2]
    in_specs = [pl.BlockSpec((1, 4, 3, NB, NB), lambda e, *_: (e, 0, 0, 0, 0))]
    for f in range(4):
        in_specs.append(
            pl.BlockSpec((1, 3, NB, NB), lambda e, s, h, p, i, t, f=f: (p[e * 4 + f], 0, 0, 0))
        )
    in_specs.append(pl.BlockSpec((1, NB, width), lambda e, *_: (e, 0, 0)))
    return pl.pallas_call(
        face_kernel,
        grid_spec=pltpu.PrefetchScalarGridSpec(
            num_scalar_prefetch=5,
            grid=(row_blocks,),
            in_specs=in_specs,
            out_specs=[
                pl.BlockSpec((1, 2, NB, NB), lambda e, *_: (e, 0, 0, 0)),
                pl.BlockSpec((1, NB, NB), lambda e, *_: (e, 0, 0)),
                pl.BlockSpec((1, NB, width), lambda e, *_: (e, 0, 0)),
                pl.BlockSpec((room, NB, NB), lambda e, *_: (0, 0, 0)),
            ],
            scratch_shapes=[pltpu.VMEM((NB, width), F32)],
        ),
        out_shape=[
            jax.ShapeDtypeStruct((row_blocks, 2, NB, NB), F32),
            jax.ShapeDtypeStruct((row_blocks, NB, NB), F32),
            jax.ShapeDtypeStruct((row_blocks, NB, width), BF16),
            jax.ShapeDtypeStruct((room, NB, NB), BF16),
        ],
        compiler_params=pltpu.CompilerParams(vmem_limit_bytes=VMEM_LIMIT),
    )(slots, held, partner, self_info, place, traces, partners, partners, partners, partners, base)


def panel_kernel(cols, transposed, kept, raw_ref, hi_ref, lo_ref, pivot_ref, out_ref):
    q, t = pl.program_id(0), pl.program_id(1)
    per = raw_ref.shape[2]
    blocks = pl.num_programs(1) * per
    first = q * blocks + t * per
    count = pl.num_programs(0) * blocks

    def masked(k, parts):
        return jnp.concatenate(
            [
                jnp.where(kept[k * count + first + i] == 1, parts[i], jnp.zeros_like(parts[i]))
                for i in range(per)
            ],
            axis=0,
        )

    def raw(k, i):
        pieces = []
        for b in range(k * PB, (k + 1) * PB):
            at = (b // cols) * NB
            pieces.append(raw_ref[0, b % cols, i, :, at : at + NB])
        return jnp.concatenate(pieces, axis=1)

    def scaled(k, v):
        w = jnp.dot(v, hi_ref[k], preferred_element_type=F32)
        return (w + jnp.dot(v, lo_ref[k], preferred_element_type=F32)).astype(BF16)

    v0 = masked(0, [raw(0, i) for i in range(per)])
    w0 = scaled(0, v0)
    taken = jnp.dot(w0, pivot_ref[...], preferred_element_type=F32)
    v1 = masked(
        1,
        [
            (raw(1, i).astype(F32) - taken[i * NB : (i + 1) * NB]).astype(BF16)
            for i in range(per)
        ],
    )
    if transposed:
        out_ref[:PW, :] = v0.T
        out_ref[PW:, :] = v1.T
    else:
        out_ref[:, :PW] = w0
        out_ref[:, PW:] = scaled(1, v1)


def panels(raw, kept, hi, lo, pivot_rows, transposed):
    groups, cols, row_blocks, _, width = raw.shape
    per = 4
    steps = row_blocks // per
    total = groups * row_blocks * NB
    whole = lambda shape: pl.BlockSpec(shape, lambda q, t, *_: (0,) * len(shape))
    if transposed:
        shape = (PANELS * PW, total)
        out_spec = pl.BlockSpec((PANELS * PW, per * NB), lambda q, t, *_: (0, q * steps + t))
    else:
        shape = (total, PANELS * PW)
        out_spec = pl.BlockSpec((per * NB, PANELS * PW), lambda q, t, *_: (q * steps + t, 0))
    return pl.pallas_call(
        functools.partial(panel_kernel, cols, transposed),
        grid_spec=pltpu.PrefetchScalarGridSpec(
            num_scalar_prefetch=1,
            grid=(groups, steps),
            in_specs=[
                pl.BlockSpec((1, cols, per, NB, width), lambda q, t, *_: (q, 0, t, 0, 0)),
                whole(hi.shape),
                whole(lo.shape),
                whole(pivot_rows.shape),
            ],
            out_specs=out_spec,
        ),
        out_shape=jax.ShapeDtypeStruct(shape, BF16),
        compiler_params=pltpu.CompilerParams(vmem_limit_bytes=VMEM_LIMIT),
    )(kept, raw, hi, lo, pivot_rows)


def update_kernel(groups, per, slots, held, self_info, a_ref, w_ref, v_ref, c_ref, d_ref, s_ref, o_ref):
    t = pl.program_id(0)
    rows, col_blocks = a_ref.shape[:2]
    per_group = col_blocks // groups
    some = 8 // groups
    w = w_ref[...]
    for first in range(0, col_blocks, 8):
        parts = []
        for h in range(groups):
            at = (h * per_group + first // groups) * NB
            parts.append(
                jnp.dot(w, v_ref[:, at : at + some * NB], preferred_element_type=F32)
            )
        slabs = [
            parts[j % groups][:, (j // groups) * NB : (j // groups + 1) * NB] for j in range(8)
        ]
        turned = jnp.transpose(jnp.stack(slabs, axis=0), (1, 0, 2))
        o_ref[:, first : first + 8, :] = a_ref[:, first : first + 8, :] - turned
    flat = o_ref.reshape(rows * col_blocks, NB)
    for i in range(per):
        e = t * per + i
        for f in range(4):

            @pl.when(held[e * 4 + f] == 1)
            def _():
                here = pl.ds(i * NB * col_blocks + slots[e * 4 + f], NB, stride=col_blocks)
                block = d_ref[i, f // 2].astype(F32) if f % 2 else c_ref[i, f // 2]
                flat[here, :] = flat[here, :] - block

        @pl.when(self_info[0] == 1)
        def _():
            here = pl.ds(i * NB * col_blocks + self_info[1 + e], NB, stride=col_blocks)
            flat[here, :] = flat[here, :] + s_ref[i]


def update(front, w, v, even, odd, self_terms, slots, held, self_info, groups):
    per = 2
    row_blocks, col_blocks = even.shape[0], front.shape[1]
    return pl.pallas_call(
        functools.partial(update_kernel, groups, per),
        grid_spec=pltpu.PrefetchScalarGridSpec(
            num_scalar_prefetch=3,
            grid=(row_blocks // per,),
            in_specs=[
                pl.BlockSpec((per * NB, col_blocks, NB), lambda t, *_: (t, 0, 0)),
                pl.BlockSpec((per * NB, PANELS * PW), lambda t, *_: (t, 0)),
                pl.BlockSpec(v.shape, lambda t, *_: (0, 0)),
                pl.BlockSpec((per, 2, NB, NB), lambda t, *_: (t, 0, 0, 0)),
                pl.BlockSpec((per, 2, NB, NB), lambda t, *_: (t, 0, 0, 0)),
                pl.BlockSpec((per, NB, NB), lambda t, *_: (t, 0, 0)),
            ],
            out_specs=pl.BlockSpec((per * NB, col_blocks, NB), lambda t, *_: (t, 0, 0)),
        ),
        out_shape=jax.ShapeDtypeStruct(front.shape, F32),
        compiler_params=pltpu.CompilerParams(vmem_limit_bytes=VMEM_LIMIT),
    )(slots, held, self_info, front, w, v, even, odd, self_terms)


def inverse_matrix(order, kinds, diagonal, pair_terms):
    ids = jnp.arange(PW, dtype=jnp.int32)
    hot = (order[:, :, None] == ids).astype(F32)
    starts = jnp.where(kinds == 1, pair_terms, 0.0)
    places = jnp.broadcast_to(ids.astype(F32), order.shape)
    wanted = jnp.stack([places, diagonal, starts], axis=1)
    found = jnp.einsum("kdi,kij->kdj", wanted, hot, precision=lax.Precision.HIGHEST)
    place, diag, pair = jnp.round(found[:, 0]).astype(jnp.int32), found[:, 1], found[:, 2]
    row, col = place[:, :, None], place[:, None, :]
    full = jnp.where(row == col, diag[:, :, None], 0.0)
    full = full + jnp.where(col == row + 1, pair[:, :, None], 0.0)
    full = full + jnp.where(row == col + 1, pair[:, None, :], 0.0)
    hi = full.astype(BF16)
    return hi, (full - hi.astype(F32)).astype(BF16)


def local(
    front_base,
    traces,
    adjacency,
    pivot_order,
    pivot_kind,
    inverse_diagonal,
    inverse_coupling,
    readers,
):
    rows, cols = lax.axis_size("row"), lax.axis_size("col")
    r, c = lax.axis_index("row"), lax.axis_index("col")
    row_blocks, col_blocks = front_base.shape[0], front_base.shape[3]
    groups = rows // cols
    panel_slots = -(-PANELS * PB // cols)
    width = panel_slots * NB

    own = traces.reshape(row_blocks, 4, 3, NB, NB)
    parts = 2
    first_even = own[0, 0::2]
    chosen = jnp.concatenate([own[:, 1::2].reshape(-1, 3, NB, NB), first_even])
    count = chosen.shape[0]
    while count * 3 * NB % (cols * 2 * parts * 16):
        count += 1
    chosen = jnp.pad(chosen, ((0, count - chosen.shape[0]), (0, 0), (0, 0), (0, 0)))
    sent = chosen.reshape(cols, 2, parts, -1, NB)
    (column_traces,) = gather(sent, rows, cols, True, 0)
    partners = column_traces.reshape(groups * count, 3, NB, NB)

    elements = jnp.arange(row_blocks, dtype=jnp.int32) * rows + r
    neighbour = jnp.take(adjacency, elements, axis=0)
    here = neighbour % cols == c
    slots = (neighbour // cols).reshape(-1)
    faces_at = jnp.arange(4, dtype=jnp.int32)
    meets = jnp.where(
        faces_at % 2 == 0,
        (neighbour // rows) * 2 + faces_at // 2,
        row_blocks * 2 + faces_at // 2,
    )
    partner = (neighbour % rows // cols) * count + meets
    needed = here & ((faces_at % 2 == 0) | (neighbour < panel_slots * cols))
    partner = jnp.where(needed, partner, 0).reshape(-1)
    held = here.astype(jnp.int32).reshape(-1)
    self_here = (r % cols == c).astype(jnp.int32)
    self_info = jnp.concatenate([self_here[None], elements // cols])

    cap = 3 * row_blocks // 4
    toward = adjacency.reshape(row_blocks, rows, 4)[:, :, 0::2] % rows
    toward = toward.transpose(0, 2, 1).reshape(row_blocks * 2, rows)
    goes = (toward[:, :, None] == jnp.arange(rows, dtype=jnp.int32)).astype(jnp.int32)
    earlier = jnp.cumsum(goes, axis=0) - goes
    rank = jnp.sum(earlier * goes, axis=2)
    crowded = jnp.any(rank >= cap)
    my_rank = lax.dynamic_index_in_dim(rank, r, 1, keepdims=False)
    my_even = neighbour[:, 0::2].reshape(-1)
    here_even = here[:, 0::2].reshape(-1)
    place = jnp.where(here_even & (my_rank < cap), my_even % rows // cols * cap + my_rank, -1)

    base = front_base[:, 0, :, :panel_slots, 0, :].reshape(row_blocks, NB, width)
    even, self_terms, raw, outgoing = faces(
        own, partners, base, slots, held, partner, self_info, place, groups * cap
    )

    every = lax.all_gather(raw[0, :, :NB], ("row", "col"), axis=0, tiled=False)
    column_raw, row_raw, incoming = gather(
        raw.reshape(2, 4, row_blocks * NB // 8, width), rows, cols, False, 1,
        outgoing.reshape(groups, cap, NB, NB),
    )

    my_odd = neighbour[:, 1::2]
    source_face = my_odd // rows * 2 + jnp.arange(2, dtype=jnp.int32)

    def from_places():
        at = (my_odd % rows // cols) * cap + rank[source_face, my_odd % rows]
        return jnp.take(incoming.reshape(groups * cap, NB, NB), at, axis=0, mode="clip")

    def from_all():
        dense = even.reshape(row_blocks * 2, NB, NB).transpose(0, 2, 1).astype(BF16)
        got = []
        for shift in range(groups):
            moves = [
                ((h * cols + a) * cols + b, ((h + shift) % groups * cols + b) * cols + a)
                for h in range(groups)
                for a in range(cols)
                for b in range(cols)
            ]
            got.append(lax.ppermute(dense, ("row", "col"), moves))
        shift = (r // cols - my_odd % rows // cols) % groups
        return jnp.stack(got)[shift, source_face]

    odd = lax.cond(crowded, from_all, from_places)

    ids = jnp.arange(rows * row_blocks, dtype=jnp.int32)
    kept = jnp.stack(
        [readers[k] * (ids >= (k + 1) * PB).astype(jnp.int32) for k in range(PANELS)]
    )
    by_row = kept.reshape(PANELS, row_blocks, rows)
    row_kept = lax.dynamic_index_in_dim(by_row, r, 2, keepdims=False)
    by_col = kept.reshape(PANELS, row_blocks, groups, cols)
    col_kept = lax.dynamic_index_in_dim(by_col, c, 3, keepdims=False).transpose(0, 2, 1)

    pivot = every.reshape(rows, cols, NB, NB)[PB : 2 * PB, :PB]
    pivot = pivot * kept[0, PB : 2 * PB].astype(BF16)[:, None, None, None]
    pivot_rows = pivot.transpose(1, 3, 0, 2).reshape(PW, PW)
    hi, lo = inverse_matrix(pivot_order, pivot_kind, inverse_diagonal, inverse_coupling)
    shape = (cols, row_blocks, NB, width)
    w = panels(row_raw.reshape((1,) + shape), row_kept.reshape(-1), hi, lo, pivot_rows, False)
    v = panels(column_raw.reshape((groups,) + shape), col_kept.reshape(-1), hi, lo, pivot_rows, True)

    front = front_base.reshape(row_blocks * NB, col_blocks, NB)
    out = update(front, w, v, even, odd, self_terms, slots, held, self_info, groups)
    return out.reshape(front_base.shape)


def solution(mesh):
    in_specs = (
        P(None, "row", None, None, "col", None),
        P(None, "row", None, None, None, None),
        P(),
        P(),
        P(),
        P(),
        P(),
        P(),
    )
    out_specs = P(None, "row", None, None, "col", None)
    return jax.shard_map(local, mesh=mesh, in_specs=in_specs, out_specs=out_specs, check_vma=False)
```

```python
import functools

import jax
import jax.numpy as jnp
from jax import lax
from jax.experimental import pallas as pl
from jax.experimental.pallas import tpu as pltpu
from jax.sharding import PartitionSpec as P

NB = 128
PW = 512
PANELS = 2
PB = PW // NB
MESH = pl.DeviceIdType.MESH
VMEM_LIMIT = 56 * 1024 * 1024
F32, BF16 = jnp.float32, jnp.bfloat16


def gather_kernel(rows, cols, parts, split, keep_row, *refs):
    if keep_row:
        (x_ref, y_ref, g_ref, l_ref, t_ref, swap_send, swap_recv, ring_send, ring_recv,
         row_send, row_recv, turn_send, turn_recv) = refs
    else:
        x_ref, g_ref, swap_send, swap_recv, ring_send, ring_recv = refs
    groups = rows // cols
    r, c = lax.axis_index("row"), lax.axis_index("col")
    s = lax.rem(r, cols)
    h = lax.div(r, cols)
    peer_row = r - s + c
    peer = (peer_row, s)
    stays = s == c

    def row_at(p):
        p = lax.rem(p + 2 * rows, rows)
        up = lax.div(p, rows // 2)
        return (1 - up) * (2 * p) + up * (2 * (rows - 1 - p) + 1)

    odd = lax.rem(r, 2)
    pos = (1 - odd) * lax.div(r, 2) + odd * (rows - 1 - lax.div(r, 2))
    beside = ((row_at(pos + 1), c), (row_at(pos - 1), c))
    pieces = [(way, part) for part in range(parts) for way in range(2)]

    barrier = pltpu.get_barrier_semaphore()
    for device in beside:
        pl.semaphore_signal(barrier, inc=1, device_id=device, device_id_type=MESH)
    greeted = 2
    if keep_row:
        for j in range(1, cols):
            pl.semaphore_signal(
                barrier, inc=1, device_id=(r, lax.rem(c + j, cols)), device_id_type=MESH
            )
        for j in range(1, groups):
            turned = lax.rem(h + j, groups) * cols + c
            pl.semaphore_signal(barrier, inc=1, device_id=(turned, s), device_id_type=MESH)
        greeted += cols - 1 + groups - 1

    @pl.when(jnp.logical_not(stays))
    def _():
        pl.semaphore_signal(barrier, inc=1, device_id=peer, device_id_type=MESH)
        pl.semaphore_wait(barrier, greeted + 1)

    @pl.when(stays)
    def _():
        pl.semaphore_wait(barrier, greeted)

    def source(way, part):
        return x_ref.at[c, way, part] if split else x_ref.at[way, part]

    def swap(way, part, slot):
        return pltpu.make_async_remote_copy(
            src_ref=source(way, part), dst_ref=g_ref.at[slot, way, part],
            send_sem=swap_send.at[way, part], recv_sem=swap_recv.at[way, part],
            device_id=peer, device_id_type=MESH,
        )

    def keep(way, part):
        return pltpu.make_async_copy(
            source(way, part), g_ref.at[r, way, part], swap_recv.at[way, part]
        )

    @pl.when(stays)
    def _():
        for piece in pieces:
            keep(*piece).start()

    @pl.when(jnp.logical_not(stays))
    def _():
        for piece in pieces:
            swap(*piece, peer_row).start()

    def along_row(j, slot):
        return pltpu.make_async_remote_copy(
            src_ref=x_ref, dst_ref=l_ref.at[slot], send_sem=row_send.at[j], recv_sem=row_recv.at[j],
            device_id=(r, lax.rem(c + j, cols)), device_id_type=MESH,
        )

    def turn(j, slot):
        k = lax.rem(h + j, groups)
        return pltpu.make_async_remote_copy(
            src_ref=y_ref.at[k], dst_ref=t_ref.at[slot], send_sem=turn_send.at[j],
            recv_sem=turn_recv.at[j], device_id=(k * cols + c, s), device_id_type=MESH,
        )

    def turn_kept():
        return pltpu.make_async_copy(y_ref.at[h], t_ref.at[h], turn_recv.at[0])

    def ring(way, part, step, behind):
        origin = row_at(pos - step - behind) if way == 0 else row_at(pos + step + behind)
        return pltpu.make_async_remote_copy(
            src_ref=g_ref.at[origin, way, part], dst_ref=g_ref.at[origin, way, part],
            send_sem=ring_send.at[way, part, step], recv_sem=ring_recv.at[way, part, step],
            device_id=beside[way], device_id_type=MESH,
        )

    for way, part in pieces:

        @pl.when(stays)
        def _():
            keep(way, part).wait()

        @pl.when(jnp.logical_not(stays))
        def _():
            swap(way, part, r).wait_recv()

        ring(way, part, 0, 0).start()
    if keep_row:
        own = pltpu.make_async_copy(x_ref, l_ref.at[c], row_recv.at[0])
        own.start()
        for j in range(1, cols):
            along_row(j, c).start()
        for j in range(1, groups):
            turn(j, h).start()

        @pl.when(stays)
        def _():
            turn_kept().start()

        @pl.when(jnp.logical_not(stays))
        def _():
            turn(0, h).start()

    for step in range(1, rows - 1):
        for way, part in pieces:
            ring(way, part, step - 1, 1).wait_recv()
            ring(way, part, step, 0).start()
    for way, part in pieces:
        ring(way, part, rows - 2, 1).wait_recv()
    for step in range(rows - 1):
        for way, part in pieces:
            ring(way, part, step, 0).wait_send()

    @pl.when(jnp.logical_not(stays))
    def _():
        for piece in pieces:
            swap(*piece, peer_row).wait_send()

    if keep_row:
        own.wait()
        for j in range(1, cols):
            along_row(j, lax.rem(c + cols - j, cols)).wait_recv()
            along_row(j, c).wait_send()
        for j in range(1, groups):
            turn(j, lax.rem(h + groups - j, groups)).wait_recv()
            turn(j, h).wait_send()

        @pl.when(stays)
        def _():
            turn_kept().wait()

        @pl.when(jnp.logical_not(stays))
        def _():
            turn(0, h).wait_recv()
            turn(0, h).wait_send()


def gather(x, rows, cols, split, identity, turned=None):
    piece = x.shape[1:] if split else x.shape
    parts = piece[1]
    out_shape = [jax.ShapeDtypeStruct((rows,) + piece, x.dtype)]
    dma = pltpu.SemaphoreType.DMA
    scratch = [dma((2, parts)), dma((2, parts)), dma((2, parts, rows - 1)), dma((2, parts, rows - 1))]
    operands = [x]
    keep_row = turned is not None
    if keep_row:
        out_shape.append(jax.ShapeDtypeStruct((cols,) + piece, x.dtype))
        out_shape.append(jax.ShapeDtypeStruct(turned.shape, turned.dtype))
        scratch += [dma((cols,)), dma((cols,)), dma((rows // cols,)), dma((rows // cols,))]
        operands.append(turned)
    moved = 2 * sum(o.size for o in out_shape)
    return pl.pallas_call(
        functools.partial(gather_kernel, rows, cols, parts, split, keep_row),
        out_shape=out_shape,
        in_specs=[pl.BlockSpec(memory_space=pl.ANY)] * len(operands),
        out_specs=[pl.BlockSpec(memory_space=pl.ANY)] * len(out_shape),
        scratch_shapes=scratch,
        compiler_params=pltpu.CompilerParams(collective_id=identity, has_side_effects=True),
        cost_estimate=pl.CostEstimate(flops=0, bytes_accessed=20 * moved, transcendentals=0),
    )(*operands)


def face_kernel(slots, held, partner, self_info, place, own_ref, p0, p1, p2, p3, a_ref, c_ref, s_ref, v_ref, t_ref, acc):
    e = pl.program_id(0)
    panel_slots = acc.shape[1] // NB
    near = a_ref.shape[1]
    flat = a_ref.reshape(NB * near, NB)
    for j in range(panel_slots):
        acc[:, j * NB : (j + 1) * NB] = flat[pl.ds(j, NB, stride=near), :]
    contract = (((0,), (0,)), ((), ()))

    def left(f):
        v, s, l = own_ref[0, f, 0], own_ref[0, f, 1], own_ref[0, f, 2]
        return jnp.concatenate([v, v, s, l], axis=0)

    def right(v, s, l):
        return jnp.concatenate([4.0 * v, -0.5 * s, -0.5 * v, 2.0 * l], axis=0)

    @pl.when(e == 0)
    def _():
        t_ref[...] = jnp.zeros_like(t_ref)

    for f, p_ref in enumerate((p0, p1, p2, p3)):
        wanted = held[e * 4 + f] == 1
        if f % 2:
            wanted = jnp.logical_and(wanted, slots[e * 4 + f] < panel_slots)

        @pl.when(wanted)
        def _():
            z = right(p_ref[0, 0], p_ref[0, 1], p_ref[0, 2])
            block = lax.dot_general(left(f), z, contract, preferred_element_type=F32)
            if f % 2 == 0:
                c_ref[0, f // 2] = block

                @pl.when(place[e * 2 + f // 2] >= 0)
                def _():
                    t_ref[place[e * 2 + f // 2]] = block.T.astype(BF16)

            for j in range(panel_slots):

                @pl.when(slots[e * 4 + f] == j)
                def _():
                    acc[:, j * NB : (j + 1) * NB] -= block

    @pl.when(self_info[0] == 1)
    def _():
        total = jnp.zeros((NB, NB), F32)
        for f in range(4):
            z = right(own_ref[0, f, 0], own_ref[0, f, 1], own_ref[0, f, 2])
            total += lax.dot_general(left(f), z, contract, preferred_element_type=F32)
        s_ref[0] = total
        for j in range(panel_slots):

            @pl.when(self_info[1 + e] == j)
            def _():
                acc[:, j * NB : (j + 1) * NB] += total

    v_ref[0] = acc[...].astype(BF16)


def faces(traces, partners, front, width, slots, held, partner, self_info, place, room):
    row_blocks = traces.shape[0]
    in_specs = [pl.BlockSpec((1, 4, 3, NB, NB), lambda e, *_: (e, 0, 0, 0, 0))]
    for f in range(4):
        in_specs.append(
            pl.BlockSpec((1, 3, NB, NB), lambda e, s, h, p, i, t, f=f: (p[e * 4 + f], 0, 0, 0))
        )
    in_specs.append(pl.BlockSpec((NB, 8, NB), lambda e, *_: (e, 0, 0)))
    return pl.pallas_call(
        face_kernel,
        grid_spec=pltpu.PrefetchScalarGridSpec(
            num_scalar_prefetch=5,
            grid=(row_blocks,),
            in_specs=in_specs,
            out_specs=[
                pl.BlockSpec((1, 2, NB, NB), lambda e, *_: (e, 0, 0, 0)),
                pl.BlockSpec((1, NB, NB), lambda e, *_: (e, 0, 0)),
                pl.BlockSpec((1, NB, width), lambda e, *_: (e, 0, 0)),
                pl.BlockSpec((room, NB, NB), lambda e, *_: (0, 0, 0)),
            ],
            scratch_shapes=[pltpu.VMEM((NB, width), F32)],
        ),
        out_shape=[
            jax.ShapeDtypeStruct((row_blocks, 2, NB, NB), F32),
            jax.ShapeDtypeStruct((row_blocks, NB, NB), F32),
            jax.ShapeDtypeStruct((row_blocks, NB, width), BF16),
            jax.ShapeDtypeStruct((room, NB, NB), BF16),
        ],
        compiler_params=pltpu.CompilerParams(vmem_limit_bytes=VMEM_LIMIT),
    )(slots, held, partner, self_info, place, traces, partners, partners, partners, partners, front)


def panel_kernel(cols, transposed, kept, pivot_kept, raw_ref, hi_ref, lo_ref, every_ref, out_ref, pivot_ref):
    q, t = pl.program_id(0), pl.program_id(1)
    per = raw_ref.shape[2]
    blocks = pl.num_programs(1) * per
    first = q * blocks + t * per
    count = pl.num_programs(0) * blocks

    @pl.when(jnp.logical_and(q == 0, t == 0))
    def _():
        for i in range(PB):
            block = jnp.concatenate([every_ref[i, b] for b in range(PB)], axis=1)
            block = jnp.where(pivot_kept[i] == 1, block, jnp.zeros_like(block))
            pivot_ref[:, i * NB : (i + 1) * NB] = block.T

    def masked(k, parts):
        return jnp.concatenate(
            [
                jnp.where(kept[k * count + first + i] == 1, parts[i], jnp.zeros_like(parts[i]))
                for i in range(per)
            ],
            axis=0,
        )

    def raw(k, i):
        pieces = []
        for b in range(k * PB, (k + 1) * PB):
            at = (b // cols) * NB
            pieces.append(raw_ref[0, b % cols, i, :, at : at + NB])
        return jnp.concatenate(pieces, axis=1)

    def scaled(k, v):
        w = jnp.dot(v, hi_ref[k], preferred_element_type=F32)
        return (w + jnp.dot(v, lo_ref[k], preferred_element_type=F32)).astype(BF16)

    v0 = masked(0, [raw(0, i) for i in range(per)])
    w0 = scaled(0, v0)
    taken = jnp.dot(w0, pivot_ref[...], preferred_element_type=F32)
    v1 = masked(
        1,
        [
            (raw(1, i).astype(F32) - taken[i * NB : (i + 1) * NB]).astype(BF16)
            for i in range(per)
        ],
    )
    if transposed:
        out_ref[:PW, :] = v0.T
        out_ref[PW:, :] = v1.T
    else:
        out_ref[:, :PW] = w0
        out_ref[:, PW:] = scaled(1, v1)


def panels(raw, kept, pivot_kept, hi, lo, every, transposed):
    groups, cols, row_blocks, _, width = raw.shape
    per = 4
    steps = row_blocks // per
    total = groups * row_blocks * NB
    whole = lambda shape: pl.BlockSpec(shape, lambda q, t, *_: (0,) * len(shape))
    if transposed:
        shape = (PANELS * PW, total)
        out_spec = pl.BlockSpec((PANELS * PW, per * NB), lambda q, t, *_: (0, q * steps + t))
    else:
        shape = (total, PANELS * PW)
        out_spec = pl.BlockSpec((per * NB, PANELS * PW), lambda q, t, *_: (q * steps + t, 0))
    return pl.pallas_call(
        functools.partial(panel_kernel, cols, transposed),
        grid_spec=pltpu.PrefetchScalarGridSpec(
            num_scalar_prefetch=2,
            grid=(groups, steps),
            in_specs=[
                pl.BlockSpec((1, cols, per, NB, width), lambda q, t, *_: (q, 0, t, 0, 0)),
                whole(hi.shape),
                whole(lo.shape),
                pl.BlockSpec((PB, cols, NB, NB), lambda q, t, *_: (1, 0, 0, 0)),
            ],
            out_specs=out_spec,
            scratch_shapes=[pltpu.VMEM((PW, PW), BF16)],
        ),
        out_shape=jax.ShapeDtypeStruct(shape, BF16),
        compiler_params=pltpu.CompilerParams(vmem_limit_bytes=VMEM_LIMIT),
    )(kept, pivot_kept, raw, hi, lo, every)


def update_kernel(groups, per, slots, held, self_info, a_ref, w_ref, v_ref, c_ref, d_ref, s_ref, o_ref):
    t = pl.program_id(0)
    rows, col_blocks = a_ref.shape[:2]
    per_group = col_blocks // groups
    some = 8 // groups
    w = w_ref[...]
    for first in range(0, col_blocks, 8):
        parts = []
        for h in range(groups):
            at = (h * per_group + first // groups) * NB
            parts.append(
                jnp.dot(w, v_ref[:, at : at + some * NB], preferred_element_type=F32)
            )
        slabs = [
            parts[j % groups][:, (j // groups) * NB : (j // groups + 1) * NB] for j in range(8)
        ]
        turned = jnp.transpose(jnp.stack(slabs, axis=0), (1, 0, 2))
        o_ref[:, first : first + 8, :] = a_ref[:, first : first + 8, :] - turned
    flat = o_ref.reshape(rows * col_blocks, NB)
    for i in range(per):
        e = t * per + i
        for f in range(4):

            @pl.when(held[e * 4 + f] == 1)
            def _():
                here = pl.ds(i * NB * col_blocks + slots[e * 4 + f], NB, stride=col_blocks)
                block = d_ref[i, f // 2].astype(F32) if f % 2 else c_ref[i, f // 2]
                flat[here, :] = flat[here, :] - block

        @pl.when(self_info[0] == 1)
        def _():
            here = pl.ds(i * NB * col_blocks + self_info[1 + e], NB, stride=col_blocks)
            flat[here, :] = flat[here, :] + s_ref[i]


def update(front, w, v, even, odd, self_terms, slots, held, self_info, groups):
    per = 2
    row_blocks, col_blocks = even.shape[0], front.shape[1]
    return pl.pallas_call(
        functools.partial(update_kernel, groups, per),
        grid_spec=pltpu.PrefetchScalarGridSpec(
            num_scalar_prefetch=3,
            grid=(row_blocks // per,),
            in_specs=[
                pl.BlockSpec((per * NB, col_blocks, NB), lambda t, *_: (t, 0, 0)),
                pl.BlockSpec((per * NB, PANELS * PW), lambda t, *_: (t, 0)),
                pl.BlockSpec(v.shape, lambda t, *_: (0, 0)),
                pl.BlockSpec((per, 2, NB, NB), lambda t, *_: (t, 0, 0, 0)),
                pl.BlockSpec((per, 2, NB, NB), lambda t, *_: (t, 0, 0, 0)),
                pl.BlockSpec((per, NB, NB), lambda t, *_: (t, 0, 0)),
            ],
            out_specs=pl.BlockSpec((per * NB, col_blocks, NB), lambda t, *_: (t, 0, 0)),
        ),
        out_shape=jax.ShapeDtypeStruct(front.shape, F32),
        compiler_params=pltpu.CompilerParams(vmem_limit_bytes=VMEM_LIMIT),
    )(slots, held, self_info, front, w, v, even, odd, self_terms)


def inverse_matrix(order, kinds, diagonal, pair_terms):
    ids = jnp.arange(PW, dtype=jnp.int32)
    hot = (order[:, :, None] == ids).astype(F32)
    starts = jnp.where(kinds == 1, pair_terms, 0.0)
    places = jnp.broadcast_to(ids.astype(F32), order.shape)
    wanted = jnp.stack([places, diagonal, starts], axis=1)
    found = jnp.einsum("kdi,kij->kdj", wanted, hot, precision=lax.Precision.HIGHEST)
    place, diag, pair = jnp.round(found[:, 0]).astype(jnp.int32), found[:, 1], found[:, 2]
    row, col = place[:, :, None], place[:, None, :]
    full = jnp.where(row == col, diag[:, :, None], 0.0)
    full = full + jnp.where(col == row + 1, pair[:, :, None], 0.0)
    full = full + jnp.where(row == col + 1, pair[:, None, :], 0.0)
    hi = full.astype(BF16)
    return hi, (full - hi.astype(F32)).astype(BF16)


def local(
    front_base,
    traces,
    adjacency,
    pivot_order,
    pivot_kind,
    inverse_diagonal,
    inverse_coupling,
    readers,
):
    rows, cols = lax.axis_size("row"), lax.axis_size("col")
    r, c = lax.axis_index("row"), lax.axis_index("col")
    row_blocks, col_blocks = front_base.shape[0], front_base.shape[3]
    groups = rows // cols
    panel_slots = -(-PANELS * PB // cols)
    width = panel_slots * NB

    own = traces.reshape(row_blocks, 4, 3, NB, NB)
    parts = 2
    first_even = own[0, 0::2]
    chosen = jnp.concatenate([own[:, 1::2].reshape(-1, 3, NB, NB), first_even])
    count = chosen.shape[0]
    while count * 3 * NB % (cols * 2 * parts * 16):
        count += 1
    chosen = jnp.pad(chosen, ((0, count - chosen.shape[0]), (0, 0), (0, 0), (0, 0)))
    sent = chosen.reshape(cols, 2, parts, -1, NB)
    (column_traces,) = gather(sent, rows, cols, True, 0)
    partners = column_traces.reshape(groups * count, 3, NB, NB)

    elements = jnp.arange(row_blocks, dtype=jnp.int32) * rows + r
    neighbour = jnp.take(adjacency, elements, axis=0)
    here = neighbour % cols == c
    slots = (neighbour // cols).reshape(-1)
    faces_at = jnp.arange(4, dtype=jnp.int32)
    meets = jnp.where(
        faces_at % 2 == 0,
        (neighbour // rows) * 2 + faces_at // 2,
        row_blocks * 2 + faces_at // 2,
    )
    partner = (neighbour % rows // cols) * count + meets
    needed = here & ((faces_at % 2 == 0) | (neighbour < panel_slots * cols))
    partner = jnp.where(needed, partner, 0).reshape(-1)
    held = here.astype(jnp.int32).reshape(-1)
    self_here = (r % cols == c).astype(jnp.int32)
    self_info = jnp.concatenate([self_here[None], elements // cols])

    cap = 3 * row_blocks // 4
    toward = adjacency.reshape(row_blocks, rows, 4)[:, :, 0::2] % rows
    toward = toward.transpose(0, 2, 1).reshape(row_blocks * 2, rows)
    goes = (toward[:, :, None] == jnp.arange(rows, dtype=jnp.int32)).astype(jnp.int32)
    earlier = jnp.cumsum(goes, axis=0) - goes
    rank = jnp.sum(earlier * goes, axis=2)
    crowded = jnp.any(rank >= cap)
    my_rank = lax.dynamic_index_in_dim(rank, r, 1, keepdims=False)
    my_even = neighbour[:, 0::2].reshape(-1)
    here_even = here[:, 0::2].reshape(-1)
    place = jnp.where(here_even & (my_rank < cap), my_even % rows // cols * cap + my_rank, -1)

    front = front_base.reshape(row_blocks * NB, col_blocks, NB)
    even, self_terms, raw, outgoing = faces(
        own, partners, front, width, slots, held, partner, self_info, place, groups * cap
    )

    every = lax.all_gather(raw[0, :, :NB], ("row", "col"), axis=0, tiled=False)
    column_raw, row_raw, incoming = gather(
        raw.reshape(2, 4, row_blocks * NB // 8, width), rows, cols, False, 1,
        outgoing.reshape(groups, cap, NB, NB),
    )

    my_odd = neighbour[:, 1::2]
    source_face = my_odd // rows * 2 + jnp.arange(2, dtype=jnp.int32)

    def from_places():
        at = (my_odd % rows // cols) * cap + rank[source_face, my_odd % rows]
        return jnp.take(incoming.reshape(groups * cap, NB, NB), at, axis=0, mode="clip")

    def from_all():
        dense = even.reshape(row_blocks * 2, NB, NB).transpose(0, 2, 1).astype(BF16)
        got = []
        for shift in range(groups):
            moves = [
                ((h * cols + a) * cols + b, ((h + shift) % groups * cols + b) * cols + a)
                for h in range(groups)
                for a in range(cols)
                for b in range(cols)
            ]
            got.append(lax.ppermute(dense, ("row", "col"), moves))
        shift = (r // cols - my_odd % rows // cols) % groups
        return jnp.stack(got)[shift, source_face]

    odd = lax.cond(crowded, from_all, from_places)

    ids = jnp.arange(rows * row_blocks, dtype=jnp.int32)
    kept = jnp.stack(
        [readers[k] * (ids >= (k + 1) * PB).astype(jnp.int32) for k in range(PANELS)]
    )
    by_row = kept.reshape(PANELS, row_blocks, rows)
    row_kept = lax.dynamic_index_in_dim(by_row, r, 2, keepdims=False)
    by_col = kept.reshape(PANELS, row_blocks, groups, cols)
    col_kept = lax.dynamic_index_in_dim(by_col, c, 3, keepdims=False).transpose(0, 2, 1)

    every = every.reshape(rows, cols, NB, NB)
    pivot_kept = kept[0, PB : 2 * PB]
    hi, lo = inverse_matrix(pivot_order, pivot_kind, inverse_diagonal, inverse_coupling)
    shape = (cols, row_blocks, NB, width)
    w = panels(row_raw.reshape((1,) + shape), row_kept.reshape(-1), pivot_kept, hi, lo, every, False)
    v = panels(column_raw.reshape((groups,) + shape), col_kept.reshape(-1), pivot_kept, hi, lo, every, True)

    out = update(front, w, v, even, odd, self_terms, slots, held, self_info, groups)
    return out.reshape(front_base.shape)


def solution(mesh):
    in_specs = (
        P(None, "row", None, None, "col", None),
        P(None, "row", None, None, None, None),
        P(),
        P(),
        P(),
        P(),
        P(),
        P(),
    )
    out_specs = P(None, "row", None, None, "col", None)
    return jax.shard_map(local, mesh=mesh, in_specs=in_specs, out_specs=out_specs, check_vma=False)
```
